512 devices in a mesh: dp: 32 (over y, z_lo), tensor: 16 (over x, z_hi, core).
Axes of the slice: x: 4, y: 4, z: 16 (z_hi: 2, z_lo: 8; z = z_hi * 8 + z_lo), core: 2. Of those that a mesh axis runs over, the one named last changes fastest.
Arguments:
- acts: bfloat16 [8192, 8192], P('dp', 'tensor'), may hold values from -6 to 6
- gate_pre: bfloat16 [8192, 28672], P('dp', 'tensor'), may hold values from -9 to 9
- up_pre: bfloat16 [8192, 28672], P('dp', 'tensor'), may hold values from -6 to 6
- hidden_grad: bfloat16 [8192, 28672], P('dp', 'tensor'), may hold values from -6 to 6
- proj_in: bfloat16 [64, 8192], P(None, 'tensor'), may hold values from -0.0625 to 0.0625
- proj_out: bfloat16 [2, 64, 28672], P(None, None, 'tensor'), may hold values from -0.0234375 to 0.0234375
- queries: bfloat16 [65536, 4096], P('dp', 'tensor'), may hold values from -0.019897461 to 0.019897461
Outputs:
- sketches: bfloat16 [64, 4096], P('dp', 'tensor')
- scores: float32 [65536, 64], P(('dp', 'tensor'))
The draws below stay inside these ranges and needn't reach their ends.
All inputs are finite; a program needn't handle non-finite values.
Results may differ from the reference program's by a relative error of at most 0.0049.
Values may be sent and summed in bfloat16 or wider, within the bound.
No kernel may reach another device: no remote copies, remote signals or barrier semaphores. Data moves between devices by JAX's collectives and lax.ppermute only.
A program may use at most 64 MiB of HBM per device.

```python
import jax
import jax.numpy as jnp
from jax import lax

D = 8192
FF = 28672
RANK = 64
SEQ_LEN = 128
SK = 4096
TOKENS = 8192
NTRAIN = 64
NQ = 65536


def with_spikes(result, rng, source, target, parts, factor):
    def block_of(axis_at):
        return (jnp.arange(result.shape[axis_at]) // (result.shape[axis_at] // parts)).reshape((-1,) + (1,) * (result.ndim - 1 - axis_at))

    first = jax.random.permutation(rng, parts)[block_of(target)]
    second = (block_of(target) + parts // 2) % parts
    return jnp.where((block_of(source) == first) | (block_of(source) == second), factor * result, result)


def steps_of(own_key, extent, pieces, smallest, largest):
    def one(dim, parts):
        draws = jax.random.uniform(jax.random.fold_in(jax.random.fold_in(own_key, 6), dim), (parts,), jnp.float32, smallest / len(pieces), largest / len(pieces))
        return jnp.repeat(jnp.exp(draws), extent[dim] // parts).reshape((-1,) + (1,) * (len(extent) - dim - 1))

    loudness = one(*pieces[0])
    for cut in pieces[1:]:
        loudness = loudness * one(*cut)
    return loudness


def centred(key, extent, spread, bound, cuts=(), kind=jnp.bfloat16):
    values = spread * jax.random.normal(key, extent, jnp.float32)
    if cuts:
        values = values * steps_of(key, extent, cuts, -0.22, 0.18)
    return jnp.clip(values, -bound, bound).astype(kind)


def noise_with(key, shape, width, bound, cuts, heavy, held_as=jnp.bfloat16):
    result = width * jax.random.normal(key, shape, jnp.float32)
    if cuts:
        result = result * steps_of(key, shape, cuts, -0.22, 0.18)
    return jnp.clip(with_spikes(result, jax.random.fold_in(key, 3), *heavy), -bound, bound).astype(held_as)


def setup_inputs(seed: int = 0) -> dict:
    splits = jax.random.split(jax.random.key(seed), 8)
    return {
        "acts": centred(splits[0], (TOKENS, D), 1.0, 6.0, ((0, 32), (1, 16))),
        "gate_pre": centred(splits[1], (TOKENS, FF), 1.5, 9.0, ((0, 32), (1, 16))),
        "up_pre": centred(splits[2], (TOKENS, FF), 1.0, 6.0, ((0, 32), (1, 16))),
        "hidden_grad": centred(splits[3], (TOKENS, FF), 1.0, 6.0, ((0, 32), (1, 16))),
        "proj_in": centred(splits[4], (RANK, D), D ** -0.5, 0.0625, ((1, 16),)),
        "proj_out": centred(splits[5], (2, RANK, FF), (2 * FF) ** -0.5, 0.0234375, ((2, 16),)),
        "queries": noise_with(splits[6], (NQ, SK), 0.003, 0.019897461, ((0, 32), (1, 16)), (1, 0, 32, 2.75)),
    }


def reference(acts, gate_pre, up_pre, hidden_grad, proj_in, proj_out, queries):
    def one_seq(index):
        start = (index * SEQ_LEN).astype(jnp.int32)
        gate = lax.dynamic_slice_in_dim(gate_pre, start, SEQ_LEN, 0).astype(jnp.float32)
        upval = lax.dynamic_slice_in_dim(up_pre, start, SEQ_LEN, 0).astype(jnp.float32)
        grad = lax.dynamic_slice_in_dim(hidden_grad, start, SEQ_LEN, 0).astype(jnp.float32)
        inputs = lax.dynamic_slice_in_dim(acts, start, SEQ_LEN, 0)
        sig = jax.nn.sigmoid(gate)
        gate_grad = (grad * upval * sig * (1.0 + gate * (1.0 - sig))).astype(jnp.bfloat16)
        up_grad = (grad * gate * sig).astype(jnp.bfloat16)
        out_proj = jnp.dot(gate_grad, proj_out[0].T, preferred_element_type=jnp.float32)
        out_proj = out_proj + jnp.dot(up_grad, proj_out[1].T, preferred_element_type=jnp.float32)
        in_proj = jnp.dot(inputs, proj_in.T, preferred_element_type=jnp.float32)
        outer = jnp.einsum("ta,tb->ab", out_proj, in_proj, precision=lax.Precision.HIGHEST)
        return outer.reshape(SK)

    sketch_full = lax.map(one_seq, jnp.arange(NTRAIN, dtype=jnp.int32))
    sketches = sketch_full.astype(jnp.bfloat16)
    scores = jnp.dot(queries, sketches.T, preferred_element_type=jnp.float32)
    return sketches, scores
```

```python
import jax
import jax.numpy as jnp
from jax import lax
from jax.sharding import Mesh, PartitionSpec as P

SEQ_LEN = 128
COLS = ("pair", "core")


def contract(left, right):
    return lax.dot_general(
        left, right, (((1,), (1,)), ((), ())), preferred_element_type=jnp.float32
    )


def exchange(blocks, axes):
    return lax.all_to_all(blocks, axes, split_axis=0, concat_axis=0, tiled=False)


def per_device(acts, gate_pre, up_pre, hidden_grad, proj_in, proj_out, queries):
    rank = proj_in.shape[0]
    tok = acts.shape[0]
    seqs = tok // SEQ_LEN
    n_dp, n_pair = lax.axis_size("dp"), lax.axis_size("pair")
    wide = rank // n_pair
    half = rank // 2
    gate = gate_pre.astype(jnp.float32)
    upval = up_pre.astype(jnp.float32)
    grad = hidden_grad.astype(jnp.float32)
    sig = jax.nn.sigmoid(gate)
    gate_grad = (grad * upval * sig * (1.0 + gate * (1.0 - sig))).astype(jnp.bfloat16)
    up_grad = (grad * gate * sig).astype(jnp.bfloat16)
    out_t = contract(proj_out[0], gate_grad) + contract(proj_out[1], up_grad)
    in_t = contract(proj_in, acts)
    out_b = out_t.astype(jnp.bfloat16).reshape(n_pair, 1, wide, tok)
    in_b = in_t.astype(jnp.bfloat16).reshape(1, 2, half, tok)
    parts = jnp.concatenate(
        [
            jnp.broadcast_to(out_b, (n_pair, 2, wide, tok)),
            jnp.broadcast_to(in_b, (n_pair, 2, half, tok)),
        ],
        axis=2,
    ).reshape(2 * n_pair, wide + half, tok)
    got = exchange(parts, COLS)
    total = jnp.sum(got.astype(jnp.float32), axis=0)
    outs = total[:wide].reshape(wide, seqs, SEQ_LEN)
    ins = total[wide:].reshape(half, seqs, SEQ_LEN)
    block = jnp.einsum("ast,bst->sab", outs, ins, precision=lax.Precision.HIGHEST)
    block = block.astype(jnp.bfloat16).reshape(seqs, 2, wide // 2 * half)
    sends = jnp.broadcast_to(block.transpose(1, 0, 2), (n_dp, 2, seqs, wide // 2 * half))
    sends = sends.reshape(n_dp * 2, seqs, wide // 2 * half)
    all_blocks = exchange(sends, ("dp", "core"))
    all_blocks = all_blocks.reshape(n_dp, 2, seqs, wide // 2, half)
    train = all_blocks.transpose(0, 2, 3, 1, 4).reshape(n_dp * seqs, wide // 2 * rank)
    sketches = lax.dynamic_slice_in_dim(train, lax.axis_index("dp") * seqs, seqs, 0)
    n_col = 2 * n_pair
    rows = queries.shape[0] // n_col
    part = contract(train, queries).astype(jnp.bfloat16)
    part = part.reshape(n_dp * seqs, n_col, rows).transpose(1, 0, 2)
    scores = jnp.sum(exchange(part, COLS).astype(jnp.float32), axis=0).T
    return (sketches, scores)


def solution(mesh):
    n_dp, n_tensor = mesh.devices.shape
    fine = Mesh(mesh.devices.reshape(n_dp, n_tensor // 2, 2), ("dp",) + COLS)
    return jax.shard_map(
        per_device,
        mesh=fine,
        in_specs=(
            P("dp", COLS),
            P("dp", COLS),
            P("dp", COLS),
            P("dp", COLS),
            P(None, COLS),
            P(None, None, COLS),
            P("dp", COLS),
        ),
        out_specs=(P("dp", COLS), P(("dp",) + COLS, None)),
        check_vma=False,
    )
```

```python
import jax
import jax.numpy as jnp
from jax import lax
from jax.sharding import Mesh, PartitionSpec as P

SEQ_LEN = 128
COLS = ("x", "half", "core")
NEAR = ("x", "core")
SWAP = [(0, 1), (1, 0)]


def contract(left, right):
    return lax.dot_general(
        left, right, (((1,), (1,)), ((), ())), preferred_element_type=jnp.float32
    )


def exchange(blocks, axes):
    return lax.all_to_all(blocks, axes, split_axis=0, concat_axis=0, tiled=False)


def per_device(acts, gate_pre, up_pre, hidden_grad, proj_in, proj_out, queries):
    rank = proj_in.shape[0]
    tok = acts.shape[0]
    seqs = tok // SEQ_LEN
    n_dp, n_x = lax.axis_size("dp"), lax.axis_size("x")
    my_half = lax.axis_index("half")
    tall = rank // n_x
    wide = tall // 2
    half = rank // 2
    gate = gate_pre.astype(jnp.float32)
    upval = up_pre.astype(jnp.float32)
    grad = hidden_grad.astype(jnp.float32)
    sig = jax.nn.sigmoid(gate)
    gate_grad = (grad * upval * sig * (1.0 + gate * (1.0 - sig))).astype(jnp.bfloat16)
    up_grad = (grad * gate * sig).astype(jnp.bfloat16)
    out_t = contract(proj_out[0], gate_grad) + contract(proj_out[1], up_grad)
    in_t = contract(proj_in, acts)
    out_b = out_t.astype(jnp.bfloat16).reshape(n_x, 1, tall, tok)
    in_b = in_t.astype(jnp.bfloat16).reshape(1, 2, half, tok)
    parts = jnp.concatenate(
        [
            jnp.broadcast_to(out_b, (n_x, 2, tall, tok)),
            jnp.broadcast_to(in_b, (n_x, 2, half, tok)),
        ],
        axis=2,
    ).reshape(2 * n_x, tall + half, tok)
    near = jnp.sum(exchange(parts, NEAR).astype(jnp.float32), axis=0)
    far = lax.ppermute(near.astype(jnp.bfloat16), "half", SWAP)
    total = near + far.astype(jnp.float32)
    outs = lax.dynamic_slice_in_dim(total, my_half * wide, wide, 0)
    outs = outs.reshape(wide, seqs, SEQ_LEN)
    ins = total[tall:].reshape(half, seqs, SEQ_LEN)
    block = jnp.einsum("ast,bst->sab", outs, ins, precision=lax.Precision.HIGHEST)
    block = block.astype(jnp.bfloat16).reshape(seqs, 2, wide // 2 * half)
    sends = jnp.broadcast_to(block.transpose(1, 0, 2), (n_dp, 2, seqs, wide // 2 * half))
    sends = sends.reshape(n_dp * 2, seqs, wide // 2 * half)
    all_blocks = exchange(sends, ("dp", "core"))
    all_blocks = all_blocks.reshape(n_dp, 2, seqs, wide // 2, half)
    train = all_blocks.transpose(0, 2, 3, 1, 4).reshape(n_dp * seqs, wide // 2 * rank)
    sketches = lax.dynamic_slice_in_dim(train, lax.axis_index("dp") * seqs, seqs, 0)
    rows = queries.shape[0] // (4 * n_x)
    part = contract(train, queries).astype(jnp.bfloat16)
    part = part.reshape(n_dp * seqs, n_x, 2, 2, rows).transpose(1, 3, 2, 0, 4)
    part = part.reshape(2 * n_x, 2, n_dp * seqs, rows)
    near = jnp.sum(exchange(part, NEAR).astype(jnp.float32), axis=0)
    mine = lax.dynamic_index_in_dim(near, my_half, 0, keepdims=False)
    theirs = lax.dynamic_index_in_dim(near, 1 - my_half, 0, keepdims=False)
    far = lax.ppermute(theirs.astype(jnp.bfloat16), "half", SWAP)
    scores = (mine + far.astype(jnp.float32)).T
    return (sketches, scores)


def solution(mesh):
    n_dp, n_tensor = mesh.devices.shape
    fine = Mesh(mesh.devices.reshape(n_dp, n_tensor // 4, 2, 2), ("dp",) + COLS)
    return jax.shard_map(
        per_device,
        mesh=fine,
        in_specs=(
            P("dp", COLS),
            P("dp", COLS),
            P("dp", COLS),
            P("dp", COLS),
            P(None, COLS),
            P(None, None, COLS),
            P("dp", COLS),
        ),
        out_specs=(P("dp", COLS), P(("dp",) + COLS, None)),
        check_vma=False,
    )
```

```python
import functools

import jax
import jax.numpy as jnp
import numpy as np
from jax import lax
from jax.experimental import pallas as pl
from jax.experimental.pallas import tpu as pltpu
from jax.sharding import Mesh, PartitionSpec as P

SEQ_LEN = 128
COLS = ("x", "half", "core")
NEAR = ("x", "core")
SWAP = [(0, 1), (1, 0)]
VMEM = 16 * 1024 * 1024


def contract(left, right):
    return lax.dot_general(
        left, right, (((1,), (1,)), ((), ())), preferred_element_type=jnp.float32
    )


def exchange(blocks, axes):
    return lax.all_to_all(blocks, axes, split_axis=0, concat_axis=0, tiled=False)


def project_kernel(
    n_x, cuts, acts_hbm, gate_hbm, up_hbm, grad_hbm, pin_hbm, pout_hbm, parts,
    acts, gate_pre, up_pre, hidden_grad, proj_in, proj_out, gate_grad, up_grad, sems,
):
    def fetch(at, which, source, target):
        copy = pltpu.make_async_copy(source, target, sems.at[at, which])
        copy.start()
        return copy

    spans = [pl.ds(lo, hi - lo) for lo, hi in zip(cuts[:-1], cuts[1:], strict=True)]
    waits = []
    for at, span in enumerate(spans):
        waits.append(
            [
                fetch(at, 0, gate_hbm.at[:, span], gate_pre.at[:, span]),
                fetch(at, 1, grad_hbm.at[:, span], hidden_grad.at[:, span]),
                fetch(at, 2, up_hbm.at[:, span], up_pre.at[:, span]),
                fetch(at, 3, pout_hbm.at[:, :, span], proj_out.at[:, :, span]),
            ]
        )
    last = [
        fetch(len(spans), 0, acts_hbm, acts),
        fetch(len(spans), 1, pin_hbm, proj_in),
    ]
    tok = gate_pre.shape[0]
    total = None
    for at, (lo, hi) in enumerate(zip(cuts[:-1], cuts[1:], strict=True)):
        for copy in waits[at]:
            copy.wait()
        for col in range(lo, hi, 256):
            cols = slice(col, col + 256)
            for row in range(0, tok, 32):
                rows = slice(row, row + 32)
                gate = gate_pre[rows, cols].astype(jnp.float32)
                sig = 0.5 * jnp.tanh(0.5 * gate) + 0.5
                scaled = hidden_grad[rows, cols].astype(jnp.float32) * sig
                up_grad[rows, cols] = (scaled * gate).astype(jnp.bfloat16)
                slope = 1.0 + gate * (1.0 - sig)
                full = scaled * up_pre[rows, cols].astype(jnp.float32) * slope
                gate_grad[rows, cols] = full.astype(jnp.bfloat16)
            term = contract(proj_out[0, :, cols], gate_grad[:, cols])
            term += contract(proj_out[1, :, cols], up_grad[:, cols])
            total = term if total is None else total + term
    for copy in last:
        copy.wait()
    ins = contract(proj_in[...], acts[...]).astype(jnp.bfloat16)
    outs = total.astype(jnp.bfloat16)
    rank = outs.shape[0]
    tall, half = rank // n_x, rank // 2
    for x in range(n_x):
        for core in range(2):
            slot = 2 * x + core
            parts[slot, :tall] = outs[x * tall : (x + 1) * tall]
            parts[slot, tall:] = ins[core * half : (core + 1) * half]


def project(n_x, acts, gate_pre, up_pre, hidden_grad, proj_in, proj_out):
    tok, hidden = gate_pre.shape
    rank = proj_in.shape[0]
    cuts = (0,) + tuple(range(256, hidden + 1, 512))
    shape = (2 * n_x, rank // n_x + rank // 2, tok)
    given = (acts, gate_pre, up_pre, hidden_grad, proj_in, proj_out)
    held = [pltpu.VMEM(a.shape, a.dtype) for a in given]
    grads = [pltpu.VMEM((tok, hidden), jnp.bfloat16)] * 2
    return pl.pallas_call(
        functools.partial(project_kernel, n_x, cuts),
        in_specs=[pl.BlockSpec(memory_space=pltpu.HBM)] * len(given),
        out_specs=pl.BlockSpec(memory_space=pltpu.VMEM),
        out_shape=pltpu.VMEM(shape, jnp.bfloat16),
        scratch_shapes=held + grads + [pltpu.SemaphoreType.DMA((len(cuts), 4))],
        compiler_params=pltpu.CompilerParams(vmem_limit_bytes=VMEM),
    )(*[pltpu.with_memory_space_constraint(a, pltpu.HBM) for a in given])


def score_kernel(n_x, blocks, place, queries, part):
    one = jnp.dot(blocks[0], place[0], preferred_element_type=jnp.float32)
    two = jnp.dot(blocks[1], place[1], preferred_element_type=jnp.float32)
    train = (one + two).astype(jnp.bfloat16)
    rows = part.shape[3]
    for x in range(n_x):
        for half in range(2):
            at = (4 * x + 2 * half) * rows
            both = contract(train, queries[at : at + 2 * rows]).astype(jnp.bfloat16)
            part[2 * x, half] = both[:, :rows]
            part[2 * x + 1, half] = both[:, rows:]


def partial_scores(n_x, blocks, place, queries):
    n_seq = blocks.shape[1]
    rows = queries.shape[0] // (4 * n_x)
    vmem = pl.BlockSpec(memory_space=pltpu.VMEM)
    return pl.pallas_call(
        functools.partial(score_kernel, n_x),
        in_specs=[vmem, vmem, vmem],
        out_specs=vmem,
        out_shape=pltpu.VMEM((2 * n_x, 2, n_seq, rows), jnp.bfloat16),
        compiler_params=pltpu.CompilerParams(vmem_limit_bytes=VMEM),
    )(blocks, place, queries)


def per_device(acts, gate_pre, up_pre, hidden_grad, proj_in, proj_out, queries):
    rank = proj_in.shape[0]
    tok = acts.shape[0]
    seqs = tok // SEQ_LEN
    n_dp, n_x = lax.axis_size("dp"), lax.axis_size("x")
    my_half = lax.axis_index("half")
    tall = rank // n_x
    wide = tall // 2
    few = wide // 2
    half = rank // 2
    parts = project(n_x, acts, gate_pre, up_pre, hidden_grad, proj_in, proj_out)
    near = jnp.sum(exchange(parts, NEAR).astype(jnp.float32), axis=0)
    far = lax.ppermute(near.astype(jnp.bfloat16), "half", SWAP)
    total = near + far.astype(jnp.float32)
    outs = lax.dynamic_slice_in_dim(total, my_half * wide, wide, 0)
    outs = outs.reshape(wide, seqs, SEQ_LEN)
    ins = total[tall:].reshape(half, seqs, SEQ_LEN)
    block = jnp.einsum("ast,bst->sab", outs, ins, precision=lax.Precision.HIGHEST)
    block = block.astype(jnp.bfloat16).reshape(seqs, 2, few * half)
    sends = jnp.broadcast_to(block.transpose(1, 0, 2)[:, None], (2, n_dp, seqs, few * half))
    sends = sends.reshape(n_dp * 2, seqs, few * half)
    got = exchange(sends, ("core", "dp")).reshape(2, n_dp * seqs, few * half)
    src = np.arange(few * half)[:, None]
    dst = src // half * rank + src % half
    col = np.arange(few * rank)[None, :]
    place = np.stack([col == dst, col == dst + half]).astype(jnp.bfloat16)
    part = partial_scores(n_x, got, place, queries)
    near = jnp.sum(exchange(part, NEAR).astype(jnp.float32), axis=0)
    near, got = lax.optimization_barrier((near, got))
    own = lax.dynamic_slice_in_dim(got, lax.axis_index("dp") * seqs, seqs, 1)
    own = own.reshape(2, seqs, few, half).transpose(1, 2, 0, 3)
    sketches = own.reshape(seqs, few * rank)
    mine = lax.dynamic_index_in_dim(near, my_half, 0, keepdims=False)
    theirs = lax.dynamic_index_in_dim(near, 1 - my_half, 0, keepdims=False)
    far = lax.ppermute(theirs.astype(jnp.bfloat16), "half", SWAP)
    scores = (mine + far.astype(jnp.float32)).T
    return (sketches, scores)


def solution(mesh):
    n_dp, n_tensor = mesh.devices.shape
    fine = Mesh(mesh.devices.reshape(n_dp, n_tensor // 4, 2, 2), ("dp",) + COLS)
    return jax.shard_map(
        per_device,
        mesh=fine,
        in_specs=(
            P("dp", COLS),
            P("dp", COLS),
            P("dp", COLS),
            P("dp", COLS),
            P(None, COLS),
            P(None, None, COLS),
            P("dp", COLS),
        ),
        out_specs=(P("dp", COLS), P(("dp",) + COLS, None)),
        check_vma=False,
    )
```

```python
import functools

import jax
import jax.numpy as jnp
import numpy as np
from jax import lax
from jax.experimental import pallas as pl
from jax.experimental.pallas import tpu as pltpu
from jax.sharding import Mesh, PartitionSpec as P

SEQ_LEN = 128
COLS = ("x", "half", "core")
SWAP = [(0, 1), (1, 0)]
VMEM = 16 * 1024 * 1024


def contract(left, right):
    return lax.dot_general(
        left, right, (((1,), (1,)), ((), ())), preferred_element_type=jnp.float32
    )


def exchange(blocks, axes):
    return lax.all_to_all(blocks, axes, split_axis=0, concat_axis=0, tiled=False)


def project_kernel(
    n_x, cuts, acts_hbm, gate_hbm, up_hbm, grad_hbm, pin_hbm, pout_hbm, parts,
    acts, gate_pre, up_pre, hidden_grad, proj_in, proj_out, gate_grad, up_grad, sems,
):
    def fetch(at, which, source, target):
        copy = pltpu.make_async_copy(source, target, sems.at[at, which])
        copy.start()
        return copy

    spans = [pl.ds(lo, hi - lo) for lo, hi in zip(cuts[:-1], cuts[1:], strict=True)]
    waits = []
    for at, span in enumerate(spans):
        waits.append(
            [
                fetch(at, 0, gate_hbm.at[:, span], gate_pre.at[:, span]),
                fetch(at, 1, grad_hbm.at[:, span], hidden_grad.at[:, span]),
                fetch(at, 2, up_hbm.at[:, span], up_pre.at[:, span]),
                fetch(at, 3, pout_hbm.at[:, :, span], proj_out.at[:, :, span]),
            ]
        )
    last = [
        fetch(len(spans), 0, acts_hbm, acts),
        fetch(len(spans), 1, pin_hbm, proj_in),
    ]
    tok = gate_pre.shape[0]
    total = None
    for at, (lo, hi) in enumerate(zip(cuts[:-1], cuts[1:], strict=True)):
        for copy in waits[at]:
            copy.wait()
        for col in range(lo, hi, 256):
            cols = slice(col, col + 256)
            for row in range(0, tok, 32):
                rows = slice(row, row + 32)
                gate = gate_pre[rows, cols].astype(jnp.float32)
                sig = 0.5 * jnp.tanh(0.5 * gate) + 0.5
                scaled = hidden_grad[rows, cols].astype(jnp.float32) * sig
                up_grad[rows, cols] = (scaled * gate).astype(jnp.bfloat16)
                slope = 1.0 + gate * (1.0 - sig)
                full = scaled * up_pre[rows, cols].astype(jnp.float32) * slope
                gate_grad[rows, cols] = full.astype(jnp.bfloat16)
            term = contract(proj_out[0, :, cols], gate_grad[:, cols])
            term += contract(proj_out[1, :, cols], up_grad[:, cols])
            total = term if total is None else total + term
    for copy in last:
        copy.wait()
    ins = contract(proj_in[...], acts[...]).astype(jnp.bfloat16)
    outs = total.astype(jnp.bfloat16)
    rank = outs.shape[0]
    tall, half = rank // n_x, rank // 2
    for x in range(n_x):
        for core in range(2):
            slot = core * n_x + x
            parts[slot, :tall] = outs[x * tall : (x + 1) * tall]
            parts[slot, tall:] = ins[core * half : (core + 1) * half]


def project(n_x, acts, gate_pre, up_pre, hidden_grad, proj_in, proj_out):
    tok, hidden = gate_pre.shape
    rank = proj_in.shape[0]
    cuts = (0,) + tuple(range(256, hidden + 1, 512))
    shape = (2 * n_x, rank // n_x + rank // 2, tok)
    given = (acts, gate_pre, up_pre, hidden_grad, proj_in, proj_out)
    held = [pltpu.VMEM(a.shape, a.dtype) for a in given]
    grads = [pltpu.VMEM((tok, hidden), jnp.bfloat16)] * 2
    return pl.pallas_call(
        functools.partial(project_kernel, n_x, cuts),
        in_specs=[pl.BlockSpec(memory_space=pltpu.HBM)] * len(given),
        out_specs=pl.BlockSpec(memory_space=pltpu.VMEM),
        out_shape=pltpu.VMEM(shape, jnp.bfloat16),
        scratch_shapes=held + grads + [pltpu.SemaphoreType.DMA((len(cuts), 4))],
        compiler_params=pltpu.CompilerParams(vmem_limit_bytes=VMEM),
    )(*[pltpu.with_memory_space_constraint(a, pltpu.HBM) for a in given])


def score_kernel(n_x, blocks, place, queries, part):
    one = jnp.dot(blocks[0], place[0], preferred_element_type=jnp.float32)
    two = jnp.dot(blocks[1], place[1], preferred_element_type=jnp.float32)
    train = (one + two).astype(jnp.bfloat16)
    rows = part.shape[3]
    for x in range(n_x):
        for half in range(2):
            at = (4 * x + 2 * half) * rows
            both = contract(train, queries[at : at + 2 * rows]).astype(jnp.bfloat16)
            part[x, half] = both[:, :rows]
            part[n_x + x, half] = both[:, rows:]


def partial_scores(n_x, blocks, place, queries):
    n_seq = blocks.shape[1]
    rows = queries.shape[0] // (4 * n_x)
    vmem = pl.BlockSpec(memory_space=pltpu.VMEM)
    return pl.pallas_call(
        functools.partial(score_kernel, n_x),
        in_specs=[vmem, vmem, vmem],
        out_specs=vmem,
        out_shape=pltpu.VMEM((2 * n_x, 2, n_seq, rows), jnp.bfloat16),
        compiler_params=pltpu.CompilerParams(vmem_limit_bytes=VMEM),
    )(blocks, place, queries)


def own_kernel(seqs, blocks, place, sketches):
    n_seq = blocks.shape[1]
    row = lax.broadcasted_iota(jnp.int32, (8, n_seq), 0)
    seq = lax.broadcasted_iota(jnp.int32, (8, n_seq), 1)
    pick = (seq == lax.axis_index("dp") * seqs + row).astype(jnp.bfloat16)
    total = None
    for side in range(2):
        lines = jnp.dot(pick, blocks[side], preferred_element_type=jnp.float32)
        lines = lines.astype(jnp.bfloat16)
        term = jnp.dot(lines, place[side], preferred_element_type=jnp.float32)
        total = term if total is None else total + term
    sketches[...] = total[:seqs].astype(jnp.bfloat16)


def own_sketches(seqs, blocks, place):
    vmem = pl.BlockSpec(memory_space=pltpu.VMEM)
    return pl.pallas_call(
        functools.partial(own_kernel, seqs),
        in_specs=[vmem, vmem],
        out_specs=vmem,
        out_shape=jax.ShapeDtypeStruct((seqs, place.shape[2]), jnp.bfloat16),
        compiler_params=pltpu.CompilerParams(vmem_limit_bytes=VMEM),
    )(blocks, place)


def split_kernel(got, mine, theirs):
    half = lax.axis_index("half")

    def add(which):
        total = got[0, which].astype(jnp.float32)
        for x in range(1, got.shape[0]):
            total += got[x, which].astype(jnp.float32)
        return total

    mine[...] = add(half)
    theirs[...] = add(1 - half).astype(jnp.bfloat16)


def split_scores(got):
    shape = got.shape[2:]
    vmem = pl.BlockSpec(memory_space=pltpu.VMEM)
    return pl.pallas_call(
        split_kernel,
        in_specs=[vmem],
        out_specs=[vmem, vmem],
        out_shape=[
            pltpu.VMEM(shape, jnp.float32),
            jax.ShapeDtypeStruct(shape, jnp.bfloat16),
        ],
        compiler_params=pltpu.CompilerParams(vmem_limit_bytes=VMEM),
    )(got)


def per_device(acts, gate_pre, up_pre, hidden_grad, proj_in, proj_out, queries):
    rank = proj_in.shape[0]
    tok = acts.shape[0]
    seqs = tok // SEQ_LEN
    n_dp, n_x = lax.axis_size("dp"), lax.axis_size("x")
    tall = rank // n_x
    wide = tall // 2
    few = wide // 2
    half = rank // 2
    parts = project(n_x, acts, gate_pre, up_pre, hidden_grad, proj_in, proj_out)
    near = jnp.sum(exchange(parts, ("core", "x")).astype(jnp.float32), axis=0)
    far = lax.ppermute(near.astype(jnp.bfloat16), "half", SWAP)
    total = near + far.astype(jnp.float32)
    outs = lax.dynamic_slice_in_dim(total, lax.axis_index("half") * wide, wide, 0)
    outs = outs.reshape(wide, seqs, SEQ_LEN)
    ins = total[tall:].reshape(half, seqs, SEQ_LEN)
    block = jnp.einsum("ast,bst->sab", outs, ins, precision=lax.Precision.HIGHEST)
    block = block.astype(jnp.bfloat16).reshape(seqs, 2, few * half)
    sends = jnp.broadcast_to(block.transpose(1, 0, 2)[:, None], (2, n_dp, seqs, few * half))
    sends = sends.reshape(2 * n_dp, seqs, few * half)
    got = exchange(sends, ("core", "dp")).reshape(2, n_dp * seqs, few * half)
    src = np.arange(few * half)[:, None]
    dst = src // half * rank + src % half
    col = np.arange(few * rank)[None, :]
    place = np.stack([col == dst, col == dst + half]).astype(jnp.bfloat16)
    part = partial_scores(n_x, got, place, queries)
    mine, theirs = split_scores(exchange(part, ("core", "x")))
    theirs, got = lax.optimization_barrier((theirs, got))
    far = lax.ppermute(theirs, "half", SWAP)
    sketches = own_sketches(seqs, got, place)
    scores = (mine + far.astype(jnp.float32)).T
    return (sketches, scores)


def solution(mesh):
    n_dp, n_tensor = mesh.devices.shape
    fine = Mesh(mesh.devices.reshape(n_dp, n_tensor // 4, 2, 2), ("dp",) + COLS)
    return jax.shard_map(
        per_device,
        mesh=fine,
        in_specs=(
            P("dp", COLS),
            P("dp", COLS),
            P("dp", COLS),
            P("dp", COLS),
            P(None, COLS),
            P(None, None, COLS),
            P("dp", COLS),
        ),
        out_specs=(P("dp", COLS), P(("dp",) + COLS, None)),
        check_vma=False,
    )
```

```python
import functools

import jax
import jax.numpy as jnp
import numpy as np
from jax import lax
from jax.experimental import pallas as pl
from jax.experimental.pallas import tpu as pltpu
from jax.sharding import Mesh, PartitionSpec as P

SEQ_LEN = 128
DP = ("y", "low")
COLS = ("x", "half", "core")
SWAP = [(0, 1), (1, 0)]
VMEM = 16 * 1024 * 1024


def contract(left, right):
    return lax.dot_general(
        left, right, (((1,), (1,)), ((), ())), preferred_element_type=jnp.float32
    )


def exchange(blocks, axes):
    return lax.all_to_all(blocks, axes, split_axis=0, concat_axis=0, tiled=False)


def project_kernel(
    n_x, cuts, acts_hbm, gate_hbm, up_hbm, grad_hbm, pin_hbm, pout_hbm, parts,
    acts, gate_pre, up_pre, hidden_grad, proj_in, proj_out, sems,
):
    def fetch(at, which, source, target):
        copy = pltpu.make_async_copy(source, target, sems.at[at, which])
        copy.start()
        return copy

    spans = [pl.ds(lo, hi - lo) for lo, hi in zip(cuts[:-1], cuts[1:], strict=True)]
    waits, rest = [], []
    for at, span in enumerate(spans):
        waits.append(
            [
                fetch(at, 0, gate_hbm.at[:, span], gate_pre.at[:, span]),
                fetch(at, 1, grad_hbm.at[:, span], hidden_grad.at[:, span]),
                fetch(at, 2, up_hbm.at[:, span], up_pre.at[:, span]),
            ]
        )
        if at == 0:
            rest.append(fetch(at, 3, pout_hbm, proj_out))
            rest.append(fetch(len(spans), 0, acts_hbm, acts))
            rest.append(fetch(len(spans), 1, pin_hbm, proj_in))
    tok = gate_pre.shape[0]
    rank = proj_in.shape[0]
    tall, half = rank // n_x, rank // 2
    tall_rows = range(0, tok, 64)
    total = [None] * len(tall_rows)
    for at, (lo, hi) in enumerate(zip(cuts[:-1], cuts[1:], strict=True)):
        for copy in waits[at]:
            copy.wait()
        for col in range(lo, hi, 256):
            cols = slice(col, col + 256)
            for k, row in enumerate(tall_rows):
                rows = slice(row, row + 64)
                gate = gate_pre[rows, cols].astype(jnp.float32)
                sig = 0.5 * jnp.tanh(0.5 * gate) + 0.5
                scaled = hidden_grad[rows, cols].astype(jnp.float32) * sig
                up_grad = (scaled * gate).astype(jnp.bfloat16)
                slope = 1.0 + gate * (1.0 - sig)
                full = scaled * up_pre[rows, cols].astype(jnp.float32) * slope
                gate_grad = full.astype(jnp.bfloat16)
                if col == 0 and row == 0:
                    for copy in rest:
                        copy.wait()
                term = contract(gate_grad, proj_out[0, :, cols])
                term += contract(up_grad, proj_out[1, :, cols])
                total[k] = term if total[k] is None else total[k] + term
        if at == 0:
            ins = contract(proj_in[...], acts[...]).astype(jnp.bfloat16)
            for slot in range(2 * n_x):
                core = slot // n_x
                parts[slot, tall:] = ins[core * half : (core + 1) * half]
    outs = jnp.concatenate(total, axis=0).T.astype(jnp.bfloat16)
    for slot in range(2 * n_x):
        x = slot % n_x
        parts[slot, :tall] = outs[x * tall : (x + 1) * tall]


def project(n_x, acts, gate_pre, up_pre, hidden_grad, proj_in, proj_out):
    tok, hidden = gate_pre.shape
    rank = proj_in.shape[0]
    cuts = (0, 512, 1024, hidden)
    shape = (2 * n_x, rank // n_x + rank // 2, tok)
    given = (acts, gate_pre, up_pre, hidden_grad, proj_in, proj_out)
    held = [pltpu.VMEM(a.shape, a.dtype) for a in given]
    return pl.pallas_call(
        functools.partial(project_kernel, n_x, cuts),
        in_specs=[pl.BlockSpec(memory_space=pltpu.HBM)] * len(given),
        out_specs=pl.BlockSpec(memory_space=pltpu.VMEM),
        out_shape=pltpu.VMEM(shape, jnp.bfloat16),
        scratch_shapes=held + [pltpu.SemaphoreType.DMA((len(cuts), 4))],
        compiler_params=pltpu.CompilerParams(vmem_limit_bytes=VMEM),
    )(*[pltpu.with_memory_space_constraint(a, pltpu.HBM) for a in given])


def turn_kernel(wide, got, near, away):
    total = got[0].astype(jnp.float32)
    for slot in range(1, got.shape[0]):
        total += got[slot].astype(jnp.float32)
    first = lax.axis_index("half") == 0
    one, two, ins = total[:wide], total[wide : 2 * wide], total[2 * wide :]
    near[...] = jnp.concatenate([jnp.where(first, one, two), ins], axis=0)
    theirs = jnp.concatenate([jnp.where(first, two, one), ins], axis=0)
    away[...] = theirs.astype(jnp.bfloat16)


def turn(wide, got):
    vmem = pl.BlockSpec(memory_space=pltpu.VMEM)
    shape = (got.shape[1] - wide, got.shape[2])
    return pl.pallas_call(
        functools.partial(turn_kernel, wide),
        in_specs=[vmem],
        out_specs=[vmem, vmem],
        out_shape=[
            pltpu.VMEM(shape, jnp.float32),
            jax.ShapeDtypeStruct(shape, jnp.bfloat16),
        ],
        compiler_params=pltpu.CompilerParams(vmem_limit_bytes=VMEM),
    )(got)


def outer_kernel(wide, near, far, sends):
    total = near[...] + far[...].astype(jnp.float32)
    outs, ins = total[:wide], total[wide:]
    seqs, few = sends.shape[1], wide // 2
    blocks = []
    for seq in range(seqs):
        cols = slice(seq * SEQ_LEN, (seq + 1) * SEQ_LEN)
        blocks.append(
            lax.dot_general(
                outs[:, cols],
                ins[:, cols],
                (((1,), (1,)), ((), ())),
                precision=lax.Precision.HIGHEST,
                preferred_element_type=jnp.float32,
            )
        )
    n_peer = sends.shape[0] // 2
    for core in range(2):
        lines = []
        for block in blocks:
            rows = [block[core * few + a : core * few + a + 1] for a in range(few)]
            lines.append(jnp.concatenate(rows, axis=1))
        pair = jnp.concatenate(lines, axis=0)[None]
        pair = jnp.broadcast_to(pair, (n_peer, seqs, pair.shape[2]))
        sends[core * n_peer : (core + 1) * n_peer] = pair.astype(jnp.bfloat16)


def outer_blocks(wide, shape, near, far):
    vmem = pl.BlockSpec(memory_space=pltpu.VMEM)
    return pl.pallas_call(
        functools.partial(outer_kernel, wide),
        in_specs=[vmem, vmem],
        out_specs=vmem,
        out_shape=pltpu.VMEM(shape, jnp.bfloat16),
        compiler_params=pltpu.CompilerParams(vmem_limit_bytes=VMEM),
    )(near, far)


def score_kernel(n_x, blocks, place, queries, part):
    one = jnp.dot(blocks[0], place[0], preferred_element_type=jnp.float32)
    two = jnp.dot(blocks[1], place[1], preferred_element_type=jnp.float32)
    train = (one + two).astype(jnp.bfloat16)
    rows = part.shape[3]
    for x in range(n_x):
        for half in range(2):
            at = (4 * x + 2 * half) * rows
            both = contract(train, queries[at : at + 2 * rows]).astype(jnp.bfloat16)
            part[x, half] = both[:, :rows]
            part[n_x + x, half] = both[:, rows:]


def partial_scores(n_x, blocks, place, queries):
    n_seq = blocks.shape[1]
    rows = queries.shape[0] // (4 * n_x)
    vmem = pl.BlockSpec(memory_space=pltpu.VMEM)
    return pl.pallas_call(
        functools.partial(score_kernel, n_x),
        in_specs=[vmem, vmem, vmem],
        out_specs=vmem,
        out_shape=pltpu.VMEM((2 * n_x, 2, n_seq, rows), jnp.bfloat16),
        compiler_params=pltpu.CompilerParams(vmem_limit_bytes=VMEM),
    )(blocks, place, queries)


def own_kernel(seqs, blocks, place, sketches):
    n_seq = blocks.shape[1]
    row = lax.broadcasted_iota(jnp.int32, (8, n_seq), 0)
    seq = lax.broadcasted_iota(jnp.int32, (8, n_seq), 1)
    seat = lax.axis_index("y") * lax.axis_size("low") + lax.axis_index("low")
    pick = (seq == seat * seqs + row).astype(jnp.bfloat16)
    total = None
    for side in range(2):
        lines = jnp.dot(pick, blocks[side], preferred_element_type=jnp.float32)
        lines = lines.astype(jnp.bfloat16)
        term = jnp.dot(lines, place[side], preferred_element_type=jnp.float32)
        total = term if total is None else total + term
    sketches[...] = total[:seqs].astype(jnp.bfloat16)


def own_sketches(seqs, blocks, place):
    vmem = pl.BlockSpec(memory_space=pltpu.VMEM)
    return pl.pallas_call(
        functools.partial(own_kernel, seqs),
        in_specs=[vmem, vmem],
        out_specs=vmem,
        out_shape=jax.ShapeDtypeStruct((seqs, place.shape[2]), jnp.bfloat16),
        compiler_params=pltpu.CompilerParams(vmem_limit_bytes=VMEM),
    )(blocks, place)


def split_kernel(got, mine, theirs):
    half = lax.axis_index("half")

    def add(which):
        total = got[0, which].astype(jnp.float32)
        for x in range(1, got.shape[0]):
            total += got[x, which].astype(jnp.float32)
        return total

    mine[...] = add(half)
    theirs[...] = add(1 - half).astype(jnp.bfloat16)


def split_scores(got):
    shape = got.shape[2:]
    vmem = pl.BlockSpec(memory_space=pltpu.VMEM)
    return pl.pallas_call(
        split_kernel,
        in_specs=[vmem],
        out_specs=[vmem, vmem],
        out_shape=[
            pltpu.VMEM(shape, jnp.float32),
            jax.ShapeDtypeStruct(shape, jnp.bfloat16),
        ],
        compiler_params=pltpu.CompilerParams(vmem_limit_bytes=VMEM),
    )(got)


def per_device(acts, gate_pre, up_pre, hidden_grad, proj_in, proj_out, queries):
    rank = proj_in.shape[0]
    tok = acts.shape[0]
    seqs = tok // SEQ_LEN
    n_y, n_low, n_x = lax.axis_size("y"), lax.axis_size("low"), lax.axis_size("x")
    tall = rank // n_x
    wide = tall // 2
    few = wide // 2
    half = rank // 2
    parts = project(n_x, acts, gate_pre, up_pre, hidden_grad, proj_in, proj_out)
    near, away = turn(wide, exchange(parts, ("core", "x")))
    far = lax.ppermute(away, "half", SWAP)
    sends = outer_blocks(wide, (2 * n_y * n_low, seqs, few * half), near, far)
    got = exchange(sends, ("core", "y", "low"))
    got = got.reshape(2, n_y * n_low * seqs, few * half)
    src = np.arange(few * half)[:, None]
    dst = src // half * rank + src % half
    col = np.arange(few * rank)[None, :]
    place = np.stack([col == dst, col == dst + half]).astype(jnp.bfloat16)
    part = partial_scores(n_x, got, place, queries)
    mine, theirs = split_scores(exchange(part, ("core", "x")))
    theirs, got = lax.optimization_barrier((theirs, got))
    far = lax.ppermute(theirs, "half", SWAP)
    sketches = own_sketches(seqs, got, place)
    scores = (mine + far.astype(jnp.float32)).T
    return (sketches, scores)


def solution(mesh):
    n_dp, n_tensor = mesh.devices.shape
    fine = mesh.devices.reshape(n_dp // 8, 8, n_tensor // 4, 2, 2)
    fine = Mesh(fine, DP + COLS)
    return jax.shard_map(
        per_device,
        mesh=fine,
        in_specs=(
            P(DP, COLS),
            P(DP, COLS),
            P(DP, COLS),
            P(DP, COLS),
            P(None, COLS),
            P(None, None, COLS),
            P(DP, COLS),
        ),
        out_specs=(P(DP, COLS), P(DP + COLS, None)),
        check_vma=False,
    )
```

```python
import functools

import jax
import jax.numpy as jnp
from jax import lax
from jax.experimental import pallas as pl
from jax.experimental.pallas import tpu as pltpu
from jax.sharding import Mesh, PartitionSpec as P

SEQ_LEN = 128
DP = ("y", "low")
COLS = ("x", "half", "core")
SWAP = [(0, 1), (1, 0)]
VMEM = 16 * 1024 * 1024


def contract(left, right):
    return lax.dot_general(
        left, right, (((1,), (1,)), ((), ())), preferred_element_type=jnp.float32
    )


def exchange(blocks, axes):
    return lax.all_to_all(blocks, axes, split_axis=0, concat_axis=0, tiled=False)


def project_kernel(
    n_x, cuts, acts_hbm, gate_hbm, up_hbm, grad_hbm, pin_hbm, pout_hbm, parts,
    acts, gate_pre, up_pre, hidden_grad, proj_in, proj_out, sems,
):
    def fetch(at, which, source, target):
        copy = pltpu.make_async_copy(source, target, sems.at[at, which])
        copy.start()
        return copy

    spans = [pl.ds(lo, hi - lo) for lo, hi in zip(cuts[:-1], cuts[1:], strict=True)]
    waits, rest = [], []
    for at, span in enumerate(spans):
        waits.append(
            [
                fetch(at, 0, gate_hbm.at[:, span], gate_pre.at[:, span]),
                fetch(at, 1, grad_hbm.at[:, span], hidden_grad.at[:, span]),
                fetch(at, 2, up_hbm.at[:, span], up_pre.at[:, span]),
            ]
        )
        if at == 0:
            rest.append(fetch(at, 3, pout_hbm, proj_out))
            rest.append(fetch(len(spans), 0, acts_hbm, acts))
            rest.append(fetch(len(spans), 1, pin_hbm, proj_in))
    tok = gate_pre.shape[0]
    rank = proj_in.shape[0]
    tall, half = rank // n_x, rank // 2
    tall_rows = range(0, tok, 64)
    total = [None] * len(tall_rows)
    for at, (lo, hi) in enumerate(zip(cuts[:-1], cuts[1:], strict=True)):
        for copy in waits[at]:
            copy.wait()
        for col in range(lo, hi, 256):
            cols = slice(col, col + 256)
            for k, row in enumerate(tall_rows):
                rows = slice(row, row + 64)
                gate = gate_pre[rows, cols].astype(jnp.float32)
                sig = 0.5 * jnp.tanh(0.5 * gate) + 0.5
                scaled = hidden_grad[rows, cols].astype(jnp.float32) * sig
                up_grad = (scaled * gate).astype(jnp.bfloat16)
                slope = 1.0 + gate * (1.0 - sig)
                full = scaled * up_pre[rows, cols].astype(jnp.float32) * slope
                gate_grad = full.astype(jnp.bfloat16)
                if col == 0 and row == 0:
                    for copy in rest:
                        copy.wait()
                term = contract(gate_grad, proj_out[0, :, cols])
                term += contract(up_grad, proj_out[1, :, cols])
                total[k] = term if total[k] is None else total[k] + term
        if at == 0:
            ins = contract(proj_in[...], acts[...]).astype(jnp.bfloat16)
            for slot in range(2 * n_x):
                core = slot // n_x
                parts[slot, tall:] = ins[core * half : (core + 1) * half]
    outs = jnp.concatenate(total, axis=0).T.astype(jnp.bfloat16)
    for slot in range(2 * n_x):
        x = slot % n_x
        parts[slot, :tall] = outs[x * tall : (x + 1) * tall]


def project(n_x, acts, gate_pre, up_pre, hidden_grad, proj_in, proj_out):
    tok, hidden = gate_pre.shape
    rank = proj_in.shape[0]
    cuts = (0, 512, 1024, hidden)
    shape = (2 * n_x, rank // n_x + rank // 2, tok)
    given = (acts, gate_pre, up_pre, hidden_grad, proj_in, proj_out)
    held = [pltpu.VMEM(a.shape, a.dtype) for a in given]
    return pl.pallas_call(
        functools.partial(project_kernel, n_x, cuts),
        in_specs=[pl.BlockSpec(memory_space=pltpu.HBM)] * len(given),
        out_specs=pl.BlockSpec(memory_space=pltpu.VMEM),
        out_shape=pltpu.VMEM(shape, jnp.bfloat16),
        scratch_shapes=held + [pltpu.SemaphoreType.DMA((len(cuts), 4))],
        compiler_params=pltpu.CompilerParams(vmem_limit_bytes=VMEM),
    )(*[pltpu.with_memory_space_constraint(a, pltpu.HBM) for a in given])


def turn_kernel(wide, got, near, away):
    total = got[0].astype(jnp.float32)
    for slot in range(1, got.shape[0]):
        total += got[slot].astype(jnp.float32)
    first = lax.axis_index("half") == 0
    one, two, ins = total[:wide], total[wide : 2 * wide], total[2 * wide :]
    near[...] = jnp.concatenate([jnp.where(first, one, two), ins], axis=0)
    theirs = jnp.concatenate([jnp.where(first, two, one), ins], axis=0)
    away[...] = theirs.astype(jnp.bfloat16)


def turn(wide, got):
    vmem = pl.BlockSpec(memory_space=pltpu.VMEM)
    shape = (got.shape[1] - wide, got.shape[2])
    return pl.pallas_call(
        functools.partial(turn_kernel, wide),
        in_specs=[vmem],
        out_specs=[vmem, vmem],
        out_shape=[
            pltpu.VMEM(shape, jnp.float32),
            jax.ShapeDtypeStruct(shape, jnp.bfloat16),
        ],
        compiler_params=pltpu.CompilerParams(vmem_limit_bytes=VMEM),
    )(got)


def outer_kernel(wide, near, far, sends):
    total = near[...] + far[...].astype(jnp.float32)
    outs, ins = total[:wide], total[wide:]
    seqs, few = sends.shape[1], wide // 2
    blocks = []
    for seq in range(seqs):
        cols = slice(seq * SEQ_LEN, (seq + 1) * SEQ_LEN)
        blocks.append(
            lax.dot_general(
                outs[:, cols],
                ins[:, cols],
                (((1,), (1,)), ((), ())),
                precision=lax.Precision.HIGHEST,
                preferred_element_type=jnp.float32,
            )
        )
    n_peer = sends.shape[0] // 2
    for core in range(2):
        lines = []
        for block in blocks:
            rows = [block[core * few + a : core * few + a + 1] for a in range(few)]
            lines.append(jnp.concatenate(rows, axis=1))
        pair = jnp.concatenate(lines, axis=0)[None]
        pair = jnp.broadcast_to(pair, (n_peer, seqs, pair.shape[2]))
        sends[core * n_peer : (core + 1) * n_peer] = pair.astype(jnp.bfloat16)


def outer_blocks(wide, shape, near, far):
    vmem = pl.BlockSpec(memory_space=pltpu.VMEM)
    return pl.pallas_call(
        functools.partial(outer_kernel, wide),
        in_specs=[vmem, vmem],
        out_specs=vmem,
        out_shape=pltpu.VMEM(shape, jnp.bfloat16),
        compiler_params=pltpu.CompilerParams(vmem_limit_bytes=VMEM),
    )(near, far)


def interleave(few, blocks):
    half = blocks.shape[2] // few
    spans = [slice(at * half, (at + 1) * half) for at in range(few)]
    return jnp.concatenate(
        [blocks[side, :, span] for span in spans for side in range(2)], axis=1
    )


def score_kernel(n_x, few, blocks, queries, part):
    train = interleave(few, blocks)
    rows = part.shape[3]
    for x in range(n_x):
        for half in range(2):
            at = (4 * x + 2 * half) * rows
            both = contract(train, queries[at : at + 2 * rows]).astype(jnp.bfloat16)
            part[x, half] = both[:, :rows]
            part[n_x + x, half] = both[:, rows:]


def partial_scores(n_x, few, blocks, queries):
    n_seq = blocks.shape[1]
    rows = queries.shape[0] // (4 * n_x)
    vmem = pl.BlockSpec(memory_space=pltpu.VMEM)
    return pl.pallas_call(
        functools.partial(score_kernel, n_x, few),
        in_specs=[vmem, vmem],
        out_specs=vmem,
        out_shape=pltpu.VMEM((2 * n_x, 2, n_seq, rows), jnp.bfloat16),
        compiler_params=pltpu.CompilerParams(vmem_limit_bytes=VMEM),
    )(blocks, queries)


def own_kernel(seqs, few, blocks, sketches):
    n_seq = blocks.shape[1]
    row = lax.broadcasted_iota(jnp.int32, (8, n_seq), 0)
    seq = lax.broadcasted_iota(jnp.int32, (8, n_seq), 1)
    seat = lax.axis_index("y") * lax.axis_size("low") + lax.axis_index("low")
    pick = (seq == seat * seqs + row).astype(jnp.bfloat16)
    total = jnp.dot(pick, interleave(few, blocks), preferred_element_type=jnp.float32)
    sketches[...] = total[:seqs].astype(jnp.bfloat16)


def own_sketches(seqs, few, blocks):
    vmem = pl.BlockSpec(memory_space=pltpu.VMEM)
    return pl.pallas_call(
        functools.partial(own_kernel, seqs, few),
        in_specs=[vmem],
        out_specs=vmem,
        out_shape=jax.ShapeDtypeStruct((seqs, 2 * blocks.shape[2]), jnp.bfloat16),
        compiler_params=pltpu.CompilerParams(vmem_limit_bytes=VMEM),
    )(blocks)


def split_kernel(got, mine, theirs):
    half = lax.axis_index("half")

    def add(which):
        total = got[0, which].astype(jnp.float32)
        for x in range(1, got.shape[0]):
            total += got[x, which].astype(jnp.float32)
        return total

    mine[...] = add(half)
    theirs[...] = add(1 - half).astype(jnp.bfloat16)


def split_scores(got):
    shape = got.shape[2:]
    vmem = pl.BlockSpec(memory_space=pltpu.VMEM)
    return pl.pallas_call(
        split_kernel,
        in_specs=[vmem],
        out_specs=[vmem, vmem],
        out_shape=[
            pltpu.VMEM(shape, jnp.float32),
            jax.ShapeDtypeStruct(shape, jnp.bfloat16),
        ],
        compiler_params=pltpu.CompilerParams(vmem_limit_bytes=VMEM),
    )(got)


def per_device(acts, gate_pre, up_pre, hidden_grad, proj_in, proj_out, queries):
    rank = proj_in.shape[0]
    tok = acts.shape[0]
    seqs = tok // SEQ_LEN
    n_y, n_low, n_x = lax.axis_size("y"), lax.axis_size("low"), lax.axis_size("x")
    tall = rank // n_x
    wide = tall // 2
    few = wide // 2
    half = rank // 2
    parts = project(n_x, acts, gate_pre, up_pre, hidden_grad, proj_in, proj_out)
    near, away = turn(wide, exchange(parts, ("core", "x")))
    far = lax.ppermute(away, "half", SWAP)
    sends = outer_blocks(wide, (2 * n_y * n_low, seqs, few * half), near, far)
    got = exchange(sends, ("core", "y", "low"))
    got = got.reshape(2, n_y * n_low * seqs, few * half)
    part = partial_scores(n_x, few, got, queries)
    mine, theirs = split_scores(exchange(part, ("core", "x")))
    theirs, got = lax.optimization_barrier((theirs, got))
    far = lax.ppermute(theirs, "half", SWAP)
    sketches = own_sketches(seqs, few, got)
    scores = (mine + far.astype(jnp.float32)).T
    return (sketches, scores)


def solution(mesh):
    n_dp, n_tensor = mesh.devices.shape
    fine = mesh.devices.reshape(n_dp // 8, 8, n_tensor // 4, 2, 2)
    fine = Mesh(fine, DP + COLS)
    return jax.shard_map(
        per_device,
        mesh=fine,
        in_specs=(
            P(DP, COLS),
            P(DP, COLS),
            P(DP, COLS),
            P(DP, COLS),
            P(None, COLS),
            P(None, None, COLS),
            P(DP, COLS),
        ),
        out_specs=(P(DP, COLS), P(DP + COLS, None)),
        check_vma=False,
    )
```
